32 devices in a mesh: tile: 16 (over z, y, core), pgroup: 2 (over x).
Axes of the slice: x: 2, y: 2, z: 4, core: 2. Of those that a mesh axis runs over, the one named last changes fastest.
Arguments:
- echoes: bfloat16 [2048, 2, 4096], P(('pgroup', 'tile')), may hold values from -6 to 6
- offsets: int32 [16, 2048], P('tile', 'pgroup'), may hold values from 0 to 3577
- phase_index: int32 [16, 2048], P('tile', 'pgroup'), may hold values from 0 to 15
- steering: float32 [2, 16, 2048], P(None, 'tile'), may hold values from -2 to 2
- kernels: float32 [16, 8], replicated, may hold values from -2 to 2
Outputs:
- image: float32 [2, 512, 4096], P(None, 'pgroup', 'tile')
The draws below stay inside these ranges and needn't reach their ends.
All inputs are finite; a program needn't handle non-finite values.
Results may differ from the reference program's by a relative error of at most 0.0037.
Values may be sent and summed in bfloat16 or wider, within the bound.
No kernel may reach another device: no remote copies, remote signals or barrier semaphores. Data moves between devices by JAX's collectives and lax.ppermute only.
A program may use at most 64 MiB of HBM per device.

```python
import jax
import jax.numpy as jnp
from jax import lax

ROW_DEV = 256
COL_DEV = 256
PULSE_DEV = 64
R = 4096
TAPS = 8
PHASES = 16
STEPS = 4
TILES = 16
ROWS = 512
COLS = 4096
PULSES = 2048
N_PGROUP = 2


def touch_ends(drawn, own_key, smallest, top_value):
    longest = drawn.shape.index(max(drawn.shape))
    spots = []
    for shift in (0, 1):
        where = [jax.random.randint(jax.random.fold_in(own_key, axis), (), 0, length) for axis, length in enumerate(drawn.shape)]
        where[longest] = (where[longest] + shift) % drawn.shape[longest]
        spots.append(tuple(where))
    return drawn.at[spots[0]].set(smallest).at[spots[1]].set(top_value)


def levels(key, extent, shards, low, high):
    def one(position, parts):
        draws = jax.random.uniform(jax.random.fold_in(jax.random.fold_in(key, 6), position), (parts,), jnp.float32, low / len(shards), high / len(shards))
        return jnp.repeat(jnp.exp(draws), extent[position] // parts).reshape((-1,) + (1,) * (len(extent) - position - 1))

    gain = one(*shards[0])
    for cut in shards[1:]:
        gain = gain * one(*cut)
    return gain


def noise(rng, shape, width, limit, cuts=(), kind=jnp.bfloat16):
    drawn = width * jax.random.normal(rng, shape, jnp.float32)
    if cuts:
        drawn = drawn * levels(rng, shape, cuts, -0.22, 0.18)
    return jnp.clip(drawn, -limit, limit).astype(kind)


def setup_inputs(seed: int = 0) -> dict:
    seeds = jax.random.split(jax.random.key(seed), 6)
    return {
        "echoes": noise(seeds[0], (PULSES, 2, R), 1.0, 6.0, ((0, 32),)),
        "offsets": touch_ends(jax.random.randint(seeds[1], (TILES, PULSES), 0, R - ROW_DEV * N_PGROUP - TAPS + 2), jax.random.fold_in(seeds[1], 1), 0, (R - ROW_DEV * N_PGROUP - TAPS + 2) - 1).astype(jnp.int32),
        "phase_index": touch_ends(jax.random.randint(seeds[2], (TILES, PULSES), 0, PHASES), jax.random.fold_in(seeds[2], 1), 0, PHASES - 1).astype(jnp.int32),
        "steering": jnp.clip(jax.random.uniform(seeds[3], (2, TILES, PULSES), jnp.float32, -2.0, 2.0) * levels(seeds[3], (2, TILES, PULSES), ((1, 16),), -0.4, 0.0), -2.0, 2.0),
        "kernels": noise(seeds[4], (PHASES, TAPS), TAPS ** -0.5, 2.0, (), jnp.float32),
    }


def steer_table(rates, curves, columns):
    centred = jnp.arange(columns, dtype=jnp.float32) - (columns - 1) / 2.0
    angle = rates[:, None] * centred[None, :] + curves[:, None] * (centred * centred / columns)[None, :]
    return jnp.cos(angle).astype(jnp.bfloat16), jnp.sin(angle).astype(jnp.bfloat16)


def reference(echoes, offsets, phase_index, steering, kernels):
    span = ROWS + TAPS - 1
    normaliser = (STEPS * PULSE_DEV * N_PGROUP) ** -0.5

    def one_tile(tile_at):
        behind = jnp.arange(STEPS, dtype=jnp.int32)
        group_ids = jnp.arange(N_PGROUP, dtype=jnp.int32)
        blocks = group_ids[:, None] * TILES + (tile_at - behind[None, :]) % TILES
        pulse_ids = (blocks[:, :, None] * PULSE_DEV + jnp.arange(PULSE_DEV, dtype=jnp.int32)[None, None, :]).reshape(-1)
        pulse_rows = echoes[pulse_ids]
        firsts = offsets[tile_at, pulse_ids].astype(jnp.int32)
        window = jax.vmap(lambda series, first: lax.dynamic_slice_in_dim(series, first, span, 1))(pulse_rows, firsts)
        weights = kernels[phase_index[tile_at, pulse_ids]]
        summed_taps = jnp.zeros((pulse_ids.shape[0], 2, ROWS), jnp.float32)
        for tap_index in range(TAPS):
            summed_taps = summed_taps + weights[:, tap_index, None, None] * window[:, :, tap_index:tap_index + ROWS].astype(jnp.float32)
        profile = summed_taps.astype(jnp.bfloat16)
        cosine, sine = steer_table(steering[0, tile_at, pulse_ids], steering[1, tile_at, pulse_ids], COL_DEV)
        real_part = jnp.dot(profile[:, 0].T, cosine, preferred_element_type=jnp.float32) - jnp.dot(profile[:, 1].T, sine, preferred_element_type=jnp.float32)
        imag_part = jnp.dot(profile[:, 0].T, sine, preferred_element_type=jnp.float32) + jnp.dot(profile[:, 1].T, cosine, preferred_element_type=jnp.float32)
        return jnp.stack([real_part, imag_part]) * normaliser

    per_tile = lax.map(one_tile, jnp.arange(TILES, dtype=jnp.int32))
    return jnp.transpose(per_tile, (1, 2, 0, 3)).reshape(2, ROWS, COLS)
```

```python
import functools
import math

import jax
import jax.numpy as jnp
import numpy as np
from jax import lax
from jax.experimental import pallas as pl
from jax.experimental.pallas import tpu as pltpu
from jax.sharding import PartitionSpec as P

ROW_DEV = 256
COL_DEV = 256
STEPS = 4
LANES = 128


def fitted(function, terms):
    nodes = np.cos(np.pi * (np.arange(64) + 0.5) / 64) * 0.25 + 0.25
    values = function(nodes)
    scale = np.vander(nodes * nodes, terms, increasing=True)
    return [float(c) for c in np.linalg.lstsq(scale, values, rcond=None)[0]]


COSINE = fitted(lambda x: np.cos(2 * np.pi * x), 9)
SINE = fitted(lambda x: np.sin(2 * np.pi * x) / x, 8)


def horner(coefficients, z):
    total = jnp.full_like(z, coefficients[-1])
    for c in coefficients[-2::-1]:
        total = total * z + c
    return total


def whole(space=pltpu.VMEM):
    return pl.BlockSpec(memory_space=space)


def table_kernel(count, pulse_dev, steer_ref, table_ref):
    columns = COL_DEV
    u = lax.broadcasted_iota(jnp.int32, (1, columns), 1).astype(jnp.float32)
    centred = u - (columns - 1) / 2.0
    linear = centred * (1.0 / (2 * math.pi))
    square = centred * centred * (1.0 / (2 * math.pi * columns))
    for s in range(count):
        rates = steer_ref[pl.ds(s * pulse_dev, pulse_dev), 0:1]
        curves = steer_ref[pl.ds(s * pulse_dev, pulse_dev), 1:2]
        turns = rates * linear + curves * square
        x = turns - jnp.round(turns)
        z = x * x
        cosine = horner(COSINE, z)
        sine = horner(SINE, z) * x
        c16 = cosine.astype(jnp.bfloat16)
        s16 = sine.astype(jnp.bfloat16)
        m16 = (-sine).astype(jnp.bfloat16)
        at = 2 * s * pulse_dev
        table_ref[at : at + pulse_dev, :columns] = c16
        table_ref[at : at + pulse_dev, columns:] = s16
        table_ref[at + pulse_dev : at + 2 * pulse_dev, :columns] = m16
        table_ref[at + pulse_dev : at + 2 * pulse_dev, columns:] = c16


def profile_kernel(pulse_dev, rows, range_rows, taps, groups, count, where_ref, group_ref, kern_ref, echo_ref, *rest):
    outs, scratch = rest[:-1], rest[-1]
    tall = 2 * rows // LANES
    lane = lax.broadcasted_iota(jnp.int32, (tall, LANES), 1)
    top = 2 * (range_rows - rows // LANES)
    me = group_ref[0]

    for i in range(count):

        def one(p, carry, i=i):
            first = where_ref[i, 0, p]
            phase = where_ref[i, 1, p]
            a = lax.shift_right_logical(first, 7) * 2
            b = jnp.bitwise_and(first, LANES - 1)
            x0 = echo_ref[p, pl.ds(a, tall), :]
            x1 = echo_ref[p, pl.ds(a + 2, tall), :]
            x2 = echo_ref[p, pl.ds(jnp.minimum(a + 4, top), tall), :]
            keep = lane >= b
            turn = LANES - b
            w0 = pltpu.roll(jnp.where(keep, x0, x1), turn, 1)
            w1 = pltpu.roll(jnp.where(keep, x1, x2), turn, 1)
            total = kern_ref[phase, 0] * w0
            for j in range(1, taps):
                shifted = pltpu.roll(jnp.where(lane >= j, w0, w1), LANES - j, 1)
                total = total + kern_ref[phase, j] * shifted
            scratch[pl.ds(p * tall, tall), :] = total
            return carry

        lax.fori_loop(0, pulse_dev, one, 0, unroll=8)
        for f in range(groups):
            half = lax.rem(me + f, groups)
            per = ROW_DEV // LANES
            for r in range(per):
                parts = [scratch[pl.ds(half * (2 * per) + 2 * r + q, pulse_dev, stride=tall), :] for q in range(2)]
                both = jnp.concatenate(parts, axis=0)
                outs[i * groups + f][r * LANES : (r + 1) * LANES, :] = both.T.astype(jnp.bfloat16)


def project_kernel(count, normaliser, *refs):
    table_ref, out_ref = refs[count], refs[count + 1]
    left = jnp.concatenate([r[...] for r in refs[:count]], axis=1)
    image = jnp.dot(left, table_ref[...], preferred_element_type=jnp.float32)
    out_ref[0] = image[:, :COL_DEV] * normaliser
    out_ref[1] = image[:, COL_DEV:] * normaliser


def per_device(tile_count, group_count, echoes, offsets, phase_index, steering, kernels):
    pulse_dev, _, length = echoes.shape
    taps = kernels.shape[1]
    rows = ROW_DEV * group_count
    range_rows = length // LANES
    tile = lax.axis_index("tile")
    group = lax.axis_index("pgroup")
    normaliser = (STEPS * pulse_dev * group_count) ** (-0.5)

    def sent(x, by, flip):
        pairs = []
        for t in range(tile_count):
            for g in range(group_count):
                to = ((t + by) % tile_count) * group_count + (g + flip) % group_count
                pairs.append((t * group_count + g, to))
        return lax.ppermute(x, ("tile", "pgroup"), pairs)

    def where(distance):
        first = (tile - distance) % tile_count * pulse_dev
        pair = jnp.concatenate([offsets, phase_index], axis=0)
        return lax.dynamic_slice_in_dim(pair, first, pulse_dev, 1)

    asked = [sent(where(d), -d, 0) for d in range(1, STEPS)]
    spread = echoes.reshape(pulse_dev, 2, range_rows, LANES).transpose(0, 2, 1, 3).astype(jnp.float32)
    spread = spread.reshape(pulse_dev, 2 * range_rows, LANES)
    me = group.reshape(1)

    def profiles(wheres):
        count = wheres.shape[0]
        shape = jax.ShapeDtypeStruct((ROW_DEV, 2 * pulse_dev), jnp.bfloat16)
        return pl.pallas_call(
            functools.partial(profile_kernel, pulse_dev, rows, range_rows, taps, group_count, count),
            out_shape=[shape] * (count * group_count),
            in_specs=[whole(pltpu.SMEM), whole(pltpu.SMEM), whole(pltpu.SMEM), whole()],
            out_specs=[whole()] * (count * group_count),
            scratch_shapes=[pltpu.VMEM((pulse_dev * 2 * rows // LANES, LANES), jnp.float32)],
            compiler_params=pltpu.CompilerParams(vmem_limit_bytes=24 * 1024 * 1024),
            name="profiles",
        )(wheres, me, kernels, spread)

    own = profiles(where(0)[None])
    arrived = [[own[0]] + [sent(own[f], 0, f) for f in range(1, group_count)]]

    count = STEPS * group_count
    steer = steering[:, 0].reshape(2, group_count, tile_count, pulse_dev)
    picked = []
    for d in range(STEPS):
        for f in range(group_count):
            at = ((group - f) % group_count, (tile - d) % tile_count)
            piece = lax.dynamic_slice(steer, (0, at[0], at[1], 0), (2, 1, 1, pulse_dev))
            picked.append(piece.reshape(2, pulse_dev))
    picked = jnp.concatenate(picked, axis=1).T
    table = pl.pallas_call(
        functools.partial(table_kernel, count, pulse_dev),
        out_shape=jax.ShapeDtypeStruct((2 * count * pulse_dev, 2 * COL_DEV), jnp.bfloat16),
        in_specs=[whole()],
        out_specs=whole(),
        compiler_params=pltpu.CompilerParams(vmem_limit_bytes=24 * 1024 * 1024),
        name="steering_table",
    )(picked)

    far = profiles(jnp.stack(asked))
    for d in range(1, STEPS):
        arrived.append([sent(far[(d - 1) * group_count + f], d, f) for f in range(group_count)])

    left = [arrived[d][f] for d in range(STEPS) for f in range(group_count)]
    return pl.pallas_call(
        functools.partial(project_kernel, count, normaliser),
        out_shape=jax.ShapeDtypeStruct((2, ROW_DEV, COL_DEV), jnp.float32),
        in_specs=[whole()] * (count + 1),
        out_specs=whole(),
        compiler_params=pltpu.CompilerParams(vmem_limit_bytes=24 * 1024 * 1024),
        name="project",
    )(*left, table)


def solution(mesh):
    placed = (
        P(("pgroup", "tile"), None, None),
        P("tile", "pgroup"),
        P("tile", "pgroup"),
        P(None, "tile", None),
        P(),
    )
    body = functools.partial(per_device, mesh.shape["tile"], mesh.shape["pgroup"])
    return jax.shard_map(body, mesh=mesh, in_specs=placed, out_specs=P(None, "pgroup", "tile"), check_vma=False)
```

```python
import functools
import math

import jax
import jax.numpy as jnp
import numpy as np
from jax import lax
from jax.experimental import pallas as pl
from jax.experimental.pallas import tpu as pltpu
from jax.sharding import PartitionSpec as P

ROW_DEV = 256
COL_DEV = 256
STEPS = 4
LANES = 128


def fitted(function, terms):
    nodes = np.cos(np.pi * (np.arange(64) + 0.5) / 64) * 0.25 + 0.25
    values = function(nodes)
    scale = np.vander(nodes * nodes, terms, increasing=True)
    return [float(c) for c in np.linalg.lstsq(scale, values, rcond=None)[0]]


COSINE = fitted(lambda x: np.cos(2 * np.pi * x), 9)
SINE = fitted(lambda x: np.sin(2 * np.pi * x) / x, 8)


def horner(coefficients, z):
    total = jnp.full_like(z, coefficients[-1])
    for c in coefficients[-2::-1]:
        total = total * z + c
    return total


def whole(space=pltpu.VMEM):
    return pl.BlockSpec(memory_space=space)


def table_kernel(count, pulse_dev, steer_ref, table_ref):
    columns = COL_DEV
    u = lax.broadcasted_iota(jnp.int32, (1, columns), 1).astype(jnp.float32)
    centred = u - (columns - 1) / 2.0
    linear = centred * (1.0 / (2 * math.pi))
    square = centred * centred * (1.0 / (2 * math.pi * columns))
    for s in range(count):
        rates = steer_ref[pl.ds(s * pulse_dev, pulse_dev), 0:1]
        curves = steer_ref[pl.ds(s * pulse_dev, pulse_dev), 1:2]
        turns = rates * linear + curves * square
        x = turns - jnp.round(turns)
        z = x * x
        cosine = horner(COSINE, z)
        sine = horner(SINE, z) * x
        c16 = cosine.astype(jnp.bfloat16)
        s16 = sine.astype(jnp.bfloat16)
        m16 = (-sine).astype(jnp.bfloat16)
        at = 2 * s * pulse_dev
        table_ref[at : at + pulse_dev, :columns] = c16
        table_ref[at : at + pulse_dev, columns:] = s16
        table_ref[at + pulse_dev : at + 2 * pulse_dev, :columns] = m16
        table_ref[at + pulse_dev : at + 2 * pulse_dev, columns:] = c16


def profile_kernel(pulse_dev, rows, taps, phases, groups, count, at_ref, group_ref, phase_ref, kern_ref, echo_ref, *rest):
    outs, (wide, tail, turned) = rest[:-3], rest[-3:]
    tall = 2 * rows // LANES
    lane = lax.broadcasted_iota(jnp.int32, (tall, LANES), 1)
    me = group_ref[0]
    total = count * pulse_dev

    for i in range(count):

        def align(p, carry, i=i):
            k = i * pulse_dev + p
            first, last, b = at_ref[k], at_ref[total + k], at_ref[2 * total + k]
            x0 = echo_ref[pl.ds(first, tall), :]
            x1 = echo_ref[pl.ds(first + 2, tall), :]
            x2 = echo_ref[pl.ds(last, 8), :]
            keep = lane >= b
            turn = LANES - b
            wide[pl.ds(pl.multiple_of(p * tall, 8), tall), :] = pltpu.roll(jnp.where(keep, x0, x1), turn, 1)
            end = jnp.where(keep[tall - 8 :], x1[tall - 8 :], x2)
            tail[pl.ds(pl.multiple_of(p * 8, 8), 8), :] = pltpu.roll(end, turn, 1)
            return carry

        lax.fori_loop(0, pulse_dev, align, 0, unroll=32)
        for r in range(rows // LANES):
            both = [wide[pl.ds(2 * r + q, pulse_dev, stride=tall), :] for q in range(2)]
            turned[r * LANES : (r + 1) * LANES, :] = jnp.concatenate(both, axis=0).T
        both = [tail[pl.ds(6 + q, pulse_dev, stride=8), :] for q in range(2)]
        turned[rows : rows + 8, :] = jnp.concatenate(both, axis=0).T[:8]

        phase = jnp.broadcast_to(phase_ref[i], (taps, 2 * pulse_dev))
        kern = kern_ref[0]
        for h in range(1, phases):
            kern = jnp.where(phase == h, kern_ref[h], kern)
        kern = [jnp.broadcast_to(kern[j : j + 1], (16, 2 * pulse_dev)) for j in range(taps)]
        for f in range(groups):
            base = lax.rem(me + f, groups) * ROW_DEV

            def fir(m, carry, out=outs[i * groups + f], base=base):
                at = pl.multiple_of(m * 16, 16)
                summed = kern[0] * turned[pl.ds(base + at, 16), :]
                for j in range(1, taps):
                    summed = summed + kern[j] * turned[pl.ds(base + at + j, 16), :]
                out[pl.ds(at, 16), :] = summed.astype(jnp.bfloat16)
                return carry

            lax.fori_loop(0, ROW_DEV // 16, fir, 0, unroll=4)


def project_kernel(count, normaliser, *refs):
    table_ref, out_ref = refs[count], refs[count + 1]
    left = jnp.concatenate([r[...] for r in refs[:count]], axis=1)
    image = jnp.dot(left, table_ref[...], preferred_element_type=jnp.float32)
    out_ref[0] = image[:, :COL_DEV] * normaliser
    out_ref[1] = image[:, COL_DEV:] * normaliser


def per_device(tile_count, group_count, echoes, offsets, phase_index, steering, kernels):
    pulse_dev, _, length = echoes.shape
    taps = kernels.shape[1]
    rows = ROW_DEV * group_count
    range_rows = length // LANES
    tile = lax.axis_index("tile")
    group = lax.axis_index("pgroup")
    normaliser = (STEPS * pulse_dev * group_count) ** (-0.5)

    def sent(x, by, flip):
        pairs = []
        for t in range(tile_count):
            for g in range(group_count):
                to = ((t + by) % tile_count) * group_count + (g + flip) % group_count
                pairs.append((t * group_count + g, to))
        return lax.ppermute(x, ("tile", "pgroup"), pairs)

    def where(distance):
        first = (tile - distance) % tile_count * pulse_dev
        pair = jnp.concatenate([offsets, phase_index], axis=0)
        return lax.dynamic_slice_in_dim(pair, first, pulse_dev, 1)

    asked = [sent(where(d), -d, 0) for d in range(1, STEPS)]
    spread = echoes.reshape(pulse_dev, 2, range_rows, LANES).transpose(0, 2, 1, 3).astype(jnp.float32)
    spread = spread.reshape(pulse_dev * 2 * range_rows, LANES)
    me = group.reshape(1)

    phases = kernels.shape[0]
    kern = jnp.broadcast_to(kernels[:, :, None], (phases, taps, 2 * pulse_dev))

    def profiles(wheres):
        count = wheres.shape[0]
        tall = 2 * rows // LANES
        firsts = wheres[:, 0].reshape(-1)
        sample_row = 2 * (firsts // LANES)
        pulse_row = jnp.arange(count * pulse_dev, dtype=jnp.int32) % pulse_dev * (2 * range_rows)
        ends = jnp.minimum(sample_row + 4 + tall - 8, 2 * range_rows - 8)
        at = jnp.concatenate([pulse_row + sample_row, pulse_row + ends, firsts % LANES])
        phase = jnp.concatenate([wheres[:, 1:], wheres[:, 1:]], axis=2)
        shape = jax.ShapeDtypeStruct((ROW_DEV, 2 * pulse_dev), jnp.bfloat16)
        return pl.pallas_call(
            functools.partial(profile_kernel, pulse_dev, rows, taps, phases, group_count, count),
            out_shape=[shape] * (count * group_count),
            in_specs=[whole(pltpu.SMEM), whole(pltpu.SMEM), whole(), whole(), whole()],
            out_specs=[whole()] * (count * group_count),
            scratch_shapes=[
                pltpu.VMEM((pulse_dev * tall, LANES), jnp.float32),
                pltpu.VMEM((pulse_dev * 8, LANES), jnp.float32),
                pltpu.VMEM((rows + 8, 2 * pulse_dev), jnp.float32),
            ],
            compiler_params=pltpu.CompilerParams(vmem_limit_bytes=24 * 1024 * 1024),
            name="profiles",
        )(at, me, phase, kern, spread)

    own = profiles(where(0)[None])
    arrived = [[own[0]] + [sent(own[f], 0, f) for f in range(1, group_count)]]

    count = STEPS * group_count
    steer = steering[:, 0].reshape(2, group_count, tile_count, pulse_dev)
    picked = []
    for d in range(STEPS):
        for f in range(group_count):
            at = ((group - f) % group_count, (tile - d) % tile_count)
            piece = lax.dynamic_slice(steer, (0, at[0], at[1], 0), (2, 1, 1, pulse_dev))
            picked.append(piece.reshape(2, pulse_dev))
    picked = jnp.concatenate(picked, axis=1).T
    table = pl.pallas_call(
        functools.partial(table_kernel, count, pulse_dev),
        out_shape=jax.ShapeDtypeStruct((2 * count * pulse_dev, 2 * COL_DEV), jnp.bfloat16),
        in_specs=[whole()],
        out_specs=whole(),
        compiler_params=pltpu.CompilerParams(vmem_limit_bytes=24 * 1024 * 1024),
        name="steering_table",
    )(picked)

    far = profiles(jnp.stack(asked))
    for d in range(1, STEPS):
        arrived.append([sent(far[(d - 1) * group_count + f], d, f) for f in range(group_count)])

    left = [arrived[d][f] for d in range(STEPS) for f in range(group_count)]
    return pl.pallas_call(
        functools.partial(project_kernel, count, normaliser),
        out_shape=jax.ShapeDtypeStruct((2, ROW_DEV, COL_DEV), jnp.float32),
        in_specs=[whole()] * (count + 1),
        out_specs=whole(),
        compiler_params=pltpu.CompilerParams(vmem_limit_bytes=24 * 1024 * 1024),
        name="project",
    )(*left, table)


def solution(mesh):
    placed = (
        P(("pgroup", "tile"), None, None),
        P("tile", "pgroup"),
        P("tile", "pgroup"),
        P(None, "tile", None),
        P(),
    )
    body = functools.partial(per_device, mesh.shape["tile"], mesh.shape["pgroup"])
    return jax.shard_map(body, mesh=mesh, in_specs=placed, out_specs=P(None, "pgroup", "tile"), check_vma=False)
```

```python
import functools
import math

import jax
import jax.numpy as jnp
import numpy as np
from jax import lax
from jax.experimental import pallas as pl
from jax.experimental.pallas import tpu as pltpu
from jax.sharding import PartitionSpec as P

ROW_DEV = 256
COL_DEV = 256
STEPS = 4
LANES = 128


def fitted(function, terms):
    nodes = np.cos(np.pi * (np.arange(64) + 0.5) / 64) * 0.25 + 0.25
    values = function(nodes)
    scale = np.vander(nodes * nodes, terms, increasing=True)
    return [float(c) for c in np.linalg.lstsq(scale, values, rcond=None)[0]]


COSINE = fitted(lambda x: np.cos(2 * np.pi * x), 9)
SINE = fitted(lambda x: np.sin(2 * np.pi * x) / x, 8)


def horner(coefficients, z):
    total = jnp.full_like(z, coefficients[-1])
    for c in coefficients[-2::-1]:
        total = total * z + c
    return total


NOTHING = pl.CostEstimate(flops=1, bytes_accessed=1, transcendentals=0)


def whole(space=pltpu.VMEM):
    return pl.BlockSpec(memory_space=space)


def block_twice(ref, row, block, width):
    per = LANES // width
    at = pl.multiple_of(block // per * LANES, LANES)
    line = ref[pl.ds(row, 1), pl.ds(at, LANES)]
    line = pltpu.roll(line, (LANES - block % per * width) % LANES, 1)
    lane = lax.broadcasted_iota(jnp.int32, line.shape, 1)
    return jnp.where(lane < width, line, pltpu.roll(line, width, 1))


def spread_kernel(pairs_ref, spread_ref):
    step = 256

    def one(k, carry):
        at = pl.multiple_of(k * step, step)
        spread_ref[pl.ds(at, step), :] = pairs_ref[pl.ds(at, step), :].astype(jnp.float32)
        return carry

    lax.fori_loop(0, pairs_ref.shape[0] // step, one, 0)


def table_kernel(tiles, groups, pulse_dev, steer_ref, table_ref, lines):
    columns = COL_DEV
    tile, group = lax.axis_index("tile"), lax.axis_index("pgroup")
    count = STEPS * groups
    odd = lax.rem(tile, 2)
    slots = [(0, f) for f in range(groups)]
    slots += [(back, f) for f in range(groups) for back in (2, 1 + 2 * odd)]
    slots += [(3 - 2 * odd, f) for f in range(groups)]
    for s, (back, f) in enumerate(slots):
        block = lax.rem(group + (groups - f), groups) * tiles + lax.rem(tile + (tiles - back), tiles)
        for row in range(2):
            at = 2 * s + row
            lines[at : at + 1, :] = block_twice(steer_ref, row, block, pulse_dev)
    upright = lines[...].T
    u = lax.broadcasted_iota(jnp.int32, (1, columns), 1).astype(jnp.float32)
    centred = u - (columns - 1) / 2.0
    linear = centred * (1.0 / (2 * math.pi))
    square = centred * centred * (1.0 / (2 * math.pi * columns))
    for s in range(count):
        rates = upright[:pulse_dev, 2 * s : 2 * s + 1]
        curves = upright[:pulse_dev, 2 * s + 1 : 2 * s + 2]
        turns = rates * linear + curves * square
        x = turns - jnp.round(turns)
        z = x * x
        cosine = horner(COSINE, z)
        sine = horner(SINE, z) * x
        c16 = cosine.astype(jnp.bfloat16)
        s16 = sine.astype(jnp.bfloat16)
        m16 = (-sine).astype(jnp.bfloat16)
        at = 2 * s * pulse_dev
        table_ref[at : at + pulse_dev, :columns] = c16
        table_ref[at : at + pulse_dev, columns:] = s16
        table_ref[at + pulse_dev : at + 2 * pulse_dev, :columns] = m16
        table_ref[at + pulse_dev : at + 2 * pulse_dev, columns:] = c16


def profile_kernel(pulse_dev, rows, range_rows, taps, phases, groups, count, *refs):
    scalars, vectors, echoes = refs[:count], refs[count : 2 * count], refs[2 * count : 3 * count]
    kern_ref, outs, (wide, tail, turned) = refs[3 * count], refs[3 * count + 1 : -3], refs[-3:]
    tall = 2 * rows // LANES
    lane = lax.broadcasted_iota(jnp.int32, (tall, LANES), 1)
    group = lax.axis_index("pgroup")

    for i in range(count):

        def align(p, carry, where=scalars[i], echo_ref=echoes[i]):
            first = where[0, p]
            row = 2 * (first >> 7)
            b = first & (LANES - 1)
            base = p * (2 * range_rows)
            x0 = echo_ref[pl.ds(base + row, tall), :]
            x1 = echo_ref[pl.ds(base + row + 2, tall), :]
            x2 = echo_ref[pl.ds(base + jnp.minimum(row + (tall - 4), 2 * range_rows - 8), 8), :]
            keep = lane >= b
            turn = LANES - b
            wide[pl.ds(pl.multiple_of(p * tall, 8), tall), :] = pltpu.roll(jnp.where(keep, x0, x1), turn, 1)
            end = jnp.where(keep[tall - 8 :], x1[tall - 8 :], x2)
            tail[pl.ds(pl.multiple_of(p * 8, 8), 8), :] = pltpu.roll(end, turn, 1)
            return carry

        lax.fori_loop(0, pulse_dev, align, 0, unroll=32)
        for r in range(rows // LANES):
            both = [wide[pl.ds(2 * r + q, pulse_dev, stride=tall), :] for q in range(2)]
            turned[r * LANES : (r + 1) * LANES, :] = jnp.concatenate(both, axis=0).T
        both = [tail[pl.ds(6 + q, pulse_dev, stride=8), :] for q in range(2)]
        turned[rows : rows + 8, :] = jnp.concatenate(both, axis=0).T[:8]

        phase = jnp.broadcast_to(vectors[i][1:2, :], (taps, 2 * pulse_dev))
        kern = kern_ref[0]
        for h in range(1, phases):
            kern = jnp.where(phase == h, kern_ref[h], kern)
        kern = [jnp.broadcast_to(kern[j : j + 1], (16, 2 * pulse_dev)) for j in range(taps)]
        for f in range(groups):
            base = lax.rem(group + f, groups) * ROW_DEV

            def fir(m, carry, out=outs[f], base=base, i=i):
                at = pl.multiple_of(m * 16, 16)
                summed = kern[0] * turned[pl.ds(base + at, 16), :]
                for j in range(1, taps):
                    summed = summed + kern[j] * turned[pl.ds(base + at + j, 16), :]
                out[pl.ds(at, 16), i * LANES : (i + 1) * LANES] = summed.astype(jnp.bfloat16)
                return carry

            lax.fori_loop(0, ROW_DEV // 16, fir, 0, unroll=4)


def project_kernel(count, normaliser, *refs):
    table_ref, out_ref = refs[count], refs[count + 1]
    left = jnp.concatenate([r[...] for r in refs[:count]], axis=1)
    image = jnp.dot(left, table_ref[...], preferred_element_type=jnp.float32)
    out_ref[0] = image[:, :COL_DEV] * normaliser
    out_ref[1] = image[:, COL_DEV:] * normaliser


def per_device(tiles, groups, echoes, offsets, phase_index, steering, kernels):
    pulse_dev, _, length = echoes.shape
    phases, taps = kernels.shape
    rows = ROW_DEV * groups
    range_rows = length // LANES
    tall = 2 * rows // LANES
    normaliser = (STEPS * pulse_dev * groups) ** (-0.5)
    params = pltpu.CompilerParams(vmem_limit_bytes=24 * 1024 * 1024)

    tile = lax.axis_index("tile")
    odd = tile % 2

    def sent(x, even_by, odd_by, flip):
        pairs = []
        for t in range(tiles):
            for g in range(groups):
                to = ((t + (odd_by if t % 2 else even_by)) % tiles) * groups + (g + flip) % groups
                pairs.append((t * groups + g, to))
        return lax.ppermute(x, ("tile", "pgroup"), pairs)

    def in_pairs(x):
        x = x.reshape(pulse_dev, 2, range_rows, LANES).transpose(0, 2, 1, 3)
        return x.reshape(pulse_dev * range_rows * 2, LANES)

    def spread(x):
        return pl.pallas_call(
            spread_kernel,
            out_shape=jax.ShapeDtypeStruct((pulse_dev * range_rows * 2, LANES), jnp.float32),
            in_specs=[whole()],
            out_specs=whole(),
            compiler_params=params,
            cost_estimate=NOTHING,
            name="spread",
        )(in_pairs(x))

    partner = sent(echoes, 1, -1, 0)
    mine = spread(echoes)
    theirs = spread(partner)
    kern = jnp.broadcast_to(kernels[:, :, None], (phases, taps, 2 * pulse_dev))

    both = jnp.concatenate([offsets, phase_index], axis=0)

    def where(block):
        piece = lax.dynamic_slice_in_dim(both, block % tiles * pulse_dev, pulse_dev, 1)
        return jnp.concatenate([piece, piece], axis=1)

    before = tile + tiles - 2
    ask = jnp.stack([where(before), where(before + 1 - 2 * odd)])
    far_ask = where(tile + tiles - 3 + 2 * odd)
    ask, far_ask = lax.optimization_barrier((sent(ask, -2, -2, 0), sent(far_ask, -3, -1, 0)))

    def profiles(wheres, sources):
        count = len(wheres)
        shape = jax.ShapeDtypeStruct((ROW_DEV, count * 2 * pulse_dev), jnp.bfloat16)
        return pl.pallas_call(
            functools.partial(profile_kernel, pulse_dev, rows, range_rows, taps, phases, groups, count),
            out_shape=[shape] * groups,
            in_specs=[whole(pltpu.SMEM)] * count + [whole()] * (2 * count + 1),
            out_specs=[whole()] * groups,
            scratch_shapes=[
                pltpu.VMEM((pulse_dev * tall, LANES), jnp.float32),
                pltpu.VMEM((pulse_dev * 8, LANES), jnp.float32),
                pltpu.VMEM((rows + 8, 2 * pulse_dev), jnp.float32),
            ],
            compiler_params=params,
            cost_estimate=NOTHING,
            name="profiles",
        )(*wheres, *wheres, *sources, kern)

    own = profiles([where(tile)], [mine])
    *own, ask, far_ask = lax.optimization_barrier((*own, ask, far_ask))
    own = [own[0]] + [sent(own[f], 0, 0, f) for f in range(1, groups)]
    near = profiles([ask[0], ask[1]], [mine, theirs])
    near = [sent(near[f], 2, 2, f) for f in range(groups)]
    far = profiles([far_ask], [mine])
    far = [sent(far[f], 1, 3, f) for f in range(groups)]

    count = STEPS * groups
    table = pl.pallas_call(
        functools.partial(table_kernel, tiles, groups, pulse_dev),
        out_shape=jax.ShapeDtypeStruct((2 * count * pulse_dev, 2 * COL_DEV), jnp.bfloat16),
        in_specs=[whole()],
        out_specs=whole(),
        scratch_shapes=[pltpu.VMEM((2 * count, LANES), jnp.float32)],
        compiler_params=params,
        cost_estimate=NOTHING,
        name="steering_table",
    )(steering[:, 0])

    left = own + near + far
    return pl.pallas_call(
        functools.partial(project_kernel, 3 * groups, normaliser),
        out_shape=jax.ShapeDtypeStruct((2, ROW_DEV, COL_DEV), jnp.float32),
        in_specs=[whole()] * (3 * groups + 1),
        out_specs=whole(),
        compiler_params=params,
        cost_estimate=NOTHING,
        name="project",
    )(*left, table)


def solution(mesh):
    placed = (
        P(("pgroup", "tile"), None, None),
        P("tile", "pgroup"),
        P("tile", "pgroup"),
        P(None, "tile", None),
        P(),
    )
    body = functools.partial(per_device, mesh.shape["tile"], mesh.shape["pgroup"])
    return jax.shard_map(body, mesh=mesh, in_specs=placed, out_specs=P(None, "pgroup", "tile"), check_vma=False)
```

```python
import functools
import math

import jax
import jax.numpy as jnp
import numpy as np
from jax import lax
from jax.experimental import pallas as pl
from jax.experimental.pallas import tpu as pltpu
from jax.sharding import PartitionSpec as P

ROW_DEV = 256
COL_DEV = 256
STEPS = 4
LANES = 128


def fitted(function, terms):
    nodes = np.cos(np.pi * (np.arange(64) + 0.5) / 64) * 0.25 + 0.25
    values = function(nodes)
    scale = np.vander(nodes * nodes, terms, increasing=True)
    return [float(c) for c in np.linalg.lstsq(scale, values, rcond=None)[0]]


COSINE = fitted(lambda x: np.cos(2 * np.pi * x), 9)
SINE = fitted(lambda x: np.sin(2 * np.pi * x) / x, 8)


def horner(coefficients, z):
    total = jnp.full_like(z, coefficients[-1])
    for c in coefficients[-2::-1]:
        total = total * z + c
    return total


NOTHING = pl.CostEstimate(flops=1, bytes_accessed=1, transcendentals=0)


def whole(space=pltpu.VMEM):
    return pl.BlockSpec(memory_space=space)


def block_twice(ref, row, block, width):
    per = LANES // width
    at = pl.multiple_of(block // per * LANES, LANES)
    line = ref[pl.ds(row, 1), pl.ds(at, LANES)]
    line = pltpu.roll(line, (LANES - block % per * width) % LANES, 1)
    lane = lax.broadcasted_iota(jnp.int32, line.shape, 1)
    return jnp.where(lane < width, line, pltpu.roll(line, width, 1))


def spread_kernel(pairs_ref, spread_ref):
    spread_rows(pairs_ref, spread_ref)


def table_kernel(tiles, groups, pulse_dev, steer_ref, table_ref, lines):
    columns = COL_DEV
    tile, group = lax.axis_index("tile"), lax.axis_index("pgroup")
    count = STEPS * groups
    odd = lax.rem(tile, 2)
    slots = [(0, f) for f in range(groups)]
    slots += [(3 - 2 * odd, f) for f in range(groups)]
    slots += [(back, f) for f in range(groups) for back in (2, 1 + 2 * odd)]
    for s, (back, f) in enumerate(slots):
        block = lax.rem(group + (groups - f), groups) * tiles + lax.rem(tile + (tiles - back), tiles)
        for row in range(2):
            at = 2 * s + row
            lines[at : at + 1, :] = block_twice(steer_ref, row, block, pulse_dev)
    upright = lines[...].T
    u = lax.broadcasted_iota(jnp.int32, (1, columns), 1).astype(jnp.float32)
    centred = u - (columns - 1) / 2.0
    linear = centred * (1.0 / (2 * math.pi))
    square = centred * centred * (1.0 / (2 * math.pi * columns))
    for s in range(count):
        rates = upright[:pulse_dev, 2 * s : 2 * s + 1]
        curves = upright[:pulse_dev, 2 * s + 1 : 2 * s + 2]
        turns = rates * linear + curves * square
        x = turns - jnp.round(turns)
        z = x * x
        cosine = horner(COSINE, z)
        sine = horner(SINE, z) * x
        c16 = cosine.astype(jnp.bfloat16)
        s16 = sine.astype(jnp.bfloat16)
        m16 = (-sine).astype(jnp.bfloat16)
        at = 2 * s * pulse_dev
        table_ref[at : at + pulse_dev, :columns] = c16
        table_ref[at : at + pulse_dev, columns:] = s16
        table_ref[at + pulse_dev : at + 2 * pulse_dev, :columns] = m16
        table_ref[at + pulse_dev : at + 2 * pulse_dev, columns:] = c16


def spread_rows(pairs_ref, spread_ref):
    step = 256

    def one(k, carry):
        at = pl.multiple_of(k * step, step)
        spread_ref[pl.ds(at, step), :] = pairs_ref[pl.ds(at, step), :].astype(jnp.float32)
        return carry

    lax.fori_loop(0, pairs_ref.shape[0] // step, one, 0)


def profile_kernel(pulse_dev, rows, taps, phases, groups, raw, joined, *refs):
    count = len(raw)
    asks, kern_ref, refs = refs[:count], refs[count], refs[count + 1 :]
    echoes, refs = list(refs[:count]), refs[count:]
    outs, (wide, tail, turned, scalars, sems, *spare) = refs[: groups * (1 if joined else count)], refs[-5 - sum(raw) :]
    copies = [pltpu.make_async_copy(asks[i], scalars.at[i], sems.at[i]) for i in range(count)]
    for copy in copies:
        copy.start()
    tall = 2 * rows // LANES
    lane = lax.broadcasted_iota(jnp.int32, (tall, LANES), 1)
    group = lax.axis_index("pgroup")
    kerns = []
    for i in range(count):
        phase = jnp.broadcast_to(asks[i][3:4, :], (taps, 2 * pulse_dev))
        kern = kern_ref[0]
        for h in range(1, phases):
            kern = jnp.where(phase == h, kern_ref[h], kern)
        kerns.append(kern)
        if raw[i]:
            spread_rows(echoes[i], spare[0])
            echoes[i] = spare[0]

    for i in range(count):
        copies[i].wait()
        for p in range(pulse_dev):
            first, last, b = scalars[i, 0, p], scalars[i, 1, p], scalars[i, 2, p]
            x0 = echoes[i][pl.ds(first, tall), :]
            x1 = echoes[i][pl.ds(first + 2, tall), :]
            x2 = echoes[i][pl.ds(last, 8), :]
            keep = lane >= b
            turn = LANES - b
            wide[p * tall : (p + 1) * tall, :] = pltpu.roll(jnp.where(keep, x0, x1), turn, 1)
            end = jnp.where(keep[tall - 8 :], x1[tall - 8 :], x2)
            tail[p * 8 : (p + 1) * 8, :] = pltpu.roll(end, turn, 1)
        for r in range(rows // LANES):
            both = [wide[pl.ds(2 * r + q, pulse_dev, stride=tall), :] for q in range(2)]
            turned[r * LANES : (r + 1) * LANES, :] = jnp.concatenate(both, axis=0).T
        both = [tail[pl.ds(6 + q, pulse_dev, stride=8), :] for q in range(2)]
        turned[rows : rows + 8, :] = jnp.concatenate(both, axis=0).T[:8]

        kern = [jnp.broadcast_to(kerns[i][j : j + 1], (16, 2 * pulse_dev)) for j in range(taps)]
        for f in range(groups):
            base = lax.rem(group + f, groups) * ROW_DEV
            out = outs[f if joined else i * groups + f]
            lanes = slice(i * LANES, (i + 1) * LANES) if joined else slice(0, LANES)

            def fir(m, carry, out=out, lanes=lanes, base=base):
                at = pl.multiple_of(m * 16, 16)
                summed = kern[0] * turned[pl.ds(base + at, 16), :]
                for j in range(1, taps):
                    summed = summed + kern[j] * turned[pl.ds(base + at + j, 16), :]
                out[pl.ds(at, 16), lanes] = summed.astype(jnp.bfloat16)
                return carry

            lax.fori_loop(0, ROW_DEV // 16, fir, 0, unroll=4)


def project_kernel(count, first, normaliser, *refs):
    pieces, table_ref, out_ref = refs[:count], refs[count], refs[-1]
    left = jnp.concatenate([r[...] for r in pieces], axis=1)
    rows = table_ref[first : first + left.shape[1], :]
    image = jnp.dot(left, rows, preferred_element_type=jnp.float32)
    if len(refs) > count + 2:
        image = image + refs[count + 1][...]
    if normaliser is None:
        out_ref[...] = image
    else:
        out_ref[0] = image[:, :COL_DEV] * normaliser
        out_ref[1] = image[:, COL_DEV:] * normaliser


def per_device(tiles, groups, echoes, offsets, phase_index, steering, kernels):
    pulse_dev, _, length = echoes.shape
    phases, taps = kernels.shape
    rows = ROW_DEV * groups
    range_rows = length // LANES
    tall = 2 * rows // LANES
    normaliser = (STEPS * pulse_dev * groups) ** (-0.5)
    params = pltpu.CompilerParams(vmem_limit_bytes=24 * 1024 * 1024)

    tile = lax.axis_index("tile")
    odd = tile % 2

    def sent(x, even_by, odd_by, flip):
        pairs = []
        for t in range(tiles):
            for g in range(groups):
                to = ((t + (odd_by if t % 2 else even_by)) % tiles) * groups + (g + flip) % groups
                pairs.append((t * groups + g, to))
        return lax.ppermute(x, ("tile", "pgroup"), pairs)

    def in_pairs(x):
        x = x.reshape(pulse_dev, 2, range_rows, LANES).transpose(0, 2, 1, 3)
        return x.reshape(pulse_dev * range_rows * 2, LANES)

    def spread(x):
        return pl.pallas_call(
            spread_kernel,
            out_shape=jax.ShapeDtypeStruct((pulse_dev * range_rows * 2, LANES), jnp.float32),
            in_specs=[whole()],
            out_specs=whole(),
            compiler_params=params,
            cost_estimate=NOTHING,
            name="spread",
        )(in_pairs(x))

    partner = sent(echoes, 1, -1, 0)
    mine = spread(echoes)
    theirs = in_pairs(partner)
    kern = jnp.broadcast_to(kernels[:, :, None], (phases, taps, 2 * pulse_dev))

    both = jnp.concatenate([offsets, phase_index], axis=0)

    def block_of(block):
        return lax.dynamic_slice_in_dim(both, block % tiles * pulse_dev, pulse_dev, 1)

    before = tile + tiles - 2
    blocks = [before, before + 1 - 2 * odd, tile + tiles - 3 + 2 * odd, tile]
    told = jnp.stack([block_of(block) for block in blocks])
    row = 2 * (told[:, :1] // LANES)
    base = 2 * range_rows * jnp.arange(pulse_dev, dtype=jnp.int32)
    last = jnp.minimum(row + (tall - 4), 2 * range_rows - 8)
    told = jnp.concatenate([base + row, base + last, told[:, :1] % LANES, told[:, 1:]], axis=1)
    told = jnp.concatenate([told, told], axis=2)
    far_ask = sent(told[2], -3, -1, 0)
    ask = sent(told[:2], -2, -2, 0)
    far_ask, ask = lax.optimization_barrier((far_ask, ask))

    def profiles(asks, sources, raw, joined):
        count = len(sources)
        shape = jax.ShapeDtypeStruct((ROW_DEV, (count if joined else 1) * 2 * pulse_dev), jnp.bfloat16)
        outs = groups * (1 if joined else count)
        return pl.pallas_call(
            functools.partial(profile_kernel, pulse_dev, rows, taps, phases, groups, raw, joined),
            out_shape=[shape] * outs,
            in_specs=[whole()] * (2 * count + 1),
            out_specs=[whole()] * outs,
            scratch_shapes=[
                pltpu.VMEM((pulse_dev * tall, LANES), jnp.float32),
                pltpu.VMEM((pulse_dev * 8, LANES), jnp.float32),
                pltpu.VMEM((rows + 8, 2 * pulse_dev), jnp.float32),
                pltpu.SMEM((count, 4, 2 * pulse_dev), jnp.int32),
                pltpu.SemaphoreType.DMA((count,)),
            ]
            + [pltpu.VMEM((pulse_dev * 2 * range_rows, LANES), jnp.float32)] * sum(raw),
            compiler_params=params,
            cost_estimate=NOTHING,
            name="profiles",
        )(*asks, kern, *sources)

    near = profiles([ask[0], ask[1]], [mine, theirs], (False, True), True)
    near = [sent(near[f], 2, 2, f) for f in range(groups)]
    rest = profiles([far_ask, told[3]], [mine, mine], (False, False), False)
    far = [sent(rest[f], 1, 3, f) for f in range(groups)]
    own = [rest[groups]] + [sent(rest[groups + f], 0, 0, f) for f in range(1, groups)]

    count = STEPS * groups
    table = pl.pallas_call(
        functools.partial(table_kernel, tiles, groups, pulse_dev),
        out_shape=jax.ShapeDtypeStruct((2 * count * pulse_dev, 2 * COL_DEV), jnp.bfloat16),
        in_specs=[whole()],
        out_specs=whole(),
        scratch_shapes=[pltpu.VMEM((2 * count, LANES), jnp.float32)],
        compiler_params=params,
        cost_estimate=NOTHING,
        name="steering_table",
    )(steering[:, 0])

    def project(pieces, first, total, last):
        shape = (2, ROW_DEV, COL_DEV) if last else (ROW_DEV, 2 * COL_DEV)
        given = list(pieces) + [table] + ([] if total is None else [total])
        return pl.pallas_call(
            functools.partial(project_kernel, len(pieces), first, normaliser if last else None),
            out_shape=jax.ShapeDtypeStruct(shape, jnp.float32),
            in_specs=[whole()] * len(given),
            out_specs=whole(),
            compiler_params=params,
            cost_estimate=NOTHING,
            name="project",
        )(*given)

    wide = 2 * pulse_dev
    total = project(near, 2 * groups * wide, None, False)
    return project(own + far, 0, total, True)


def solution(mesh):
    placed = (
        P(("pgroup", "tile"), None, None),
        P("tile", "pgroup"),
        P("tile", "pgroup"),
        P(None, "tile", None),
        P(),
    )
    body = functools.partial(per_device, mesh.shape["tile"], mesh.shape["pgroup"])
    return jax.shard_map(body, mesh=mesh, in_specs=placed, out_specs=P(None, "pgroup", "tile"), check_vma=False)
```

```python
import functools
import math

import jax
import jax.numpy as jnp
import numpy as np
from jax import lax
from jax.experimental import pallas as pl
from jax.experimental.pallas import tpu as pltpu
from jax.sharding import PartitionSpec as P

ROW_DEV = 256
COL_DEV = 256
STEPS = 4
LANES = 128


def fitted(function, terms):
    nodes = np.cos(np.pi * (np.arange(64) + 0.5) / 64) * 0.25 + 0.25
    values = function(nodes)
    scale = np.vander(nodes * nodes, terms, increasing=True)
    return [float(c) for c in np.linalg.lstsq(scale, values, rcond=None)[0]]


COSINE = fitted(lambda x: np.cos(2 * np.pi * x), 9)
SINE = fitted(lambda x: np.sin(2 * np.pi * x) / x, 8)


def horner(coefficients, z):
    total = jnp.full_like(z, coefficients[-1])
    for c in coefficients[-2::-1]:
        total = total * z + c
    return total


NOTHING = pl.CostEstimate(flops=1, bytes_accessed=1, transcendentals=0)


def whole(space=pltpu.VMEM):
    return pl.BlockSpec(memory_space=space)


def block_twice(ref, row, block, width):
    per = LANES // width
    at = pl.multiple_of(block // per * LANES, LANES)
    line = ref[pl.ds(row, 1), pl.ds(at, LANES)]
    line = pltpu.roll(line, (LANES - block % per * width) % LANES, 1)
    lane = lax.broadcasted_iota(jnp.int32, line.shape, 1)
    return jnp.where(lane < width, line, pltpu.roll(line, width, 1))


def spread_kernel(pairs_ref, spread_ref):
    spread_rows(pairs_ref, spread_ref)


def table_kernel(tiles, groups, pulse_dev, steer_ref, table_ref, lines):
    columns = COL_DEV
    tile, group = lax.axis_index("tile"), lax.axis_index("pgroup")
    count = STEPS * groups
    odd = lax.rem(tile, 2)
    slots = [(3 - 2 * odd, f) for f in range(groups)]
    slots += [(0, f) for f in range(groups)]
    slots += [(back, f) for f in range(groups) for back in (1 + 2 * odd, 2)]
    for s, (back, f) in enumerate(slots):
        block = lax.rem(group + (groups - f), groups) * tiles + lax.rem(tile + (tiles - back), tiles)
        for row in range(2):
            at = 2 * s + row
            lines[at : at + 1, :] = block_twice(steer_ref, row, block, pulse_dev)
    upright = lines[...].T
    u = lax.broadcasted_iota(jnp.int32, (1, columns), 1).astype(jnp.float32)
    centred = u - (columns - 1) / 2.0
    linear = centred * (1.0 / (2 * math.pi))
    square = centred * centred * (1.0 / (2 * math.pi * columns))
    for s in range(count):
        rates = upright[:pulse_dev, 2 * s : 2 * s + 1]
        curves = upright[:pulse_dev, 2 * s + 1 : 2 * s + 2]
        turns = rates * linear + curves * square
        x = turns - jnp.round(turns)
        z = x * x
        cosine = horner(COSINE, z)
        sine = horner(SINE, z) * x
        c16 = cosine.astype(jnp.bfloat16)
        s16 = sine.astype(jnp.bfloat16)
        m16 = (-sine).astype(jnp.bfloat16)
        at = 2 * s * pulse_dev
        table_ref[at : at + pulse_dev, :columns] = c16
        table_ref[at : at + pulse_dev, columns:] = s16
        table_ref[at + pulse_dev : at + 2 * pulse_dev, :columns] = m16
        table_ref[at + pulse_dev : at + 2 * pulse_dev, columns:] = c16


def spread_rows(pairs_ref, spread_ref):
    step = 256

    def one(k, carry):
        at = pl.multiple_of(k * step, step)
        spread_ref[pl.ds(at, step), :] = pairs_ref[pl.ds(at, step), :].astype(jnp.float32)
        return carry

    lax.fori_loop(0, pairs_ref.shape[0] // step, one, 0)


def profile_kernel(pulse_dev, rows, taps, phases, groups, raw, joined, *refs):
    count = len(raw)
    asks, kern_ref, refs = refs[:count], refs[count], refs[count + 1 :]
    echoes, refs = list(refs[:count]), refs[count:]
    outs, (wide, tail, turned, scalars, sems, *spare) = refs[: groups * (1 if joined else count)], refs[-5 - sum(raw) :]
    copies = [pltpu.make_async_copy(asks[i], scalars.at[i], sems.at[i]) for i in range(count)]
    for copy in copies:
        copy.start()
    tall = 2 * rows // LANES
    lane = lax.broadcasted_iota(jnp.int32, (tall, LANES), 1)
    group = lax.axis_index("pgroup")
    kerns = []
    for i in range(count):
        phase = jnp.broadcast_to(asks[i][3:4, :], (taps, 2 * pulse_dev))
        kern = kern_ref[0]
        for h in range(1, phases):
            kern = jnp.where(phase == h, kern_ref[h], kern)
        kerns.append(kern)
        if raw[i]:
            spread_rows(echoes[i], spare[0])
            echoes[i] = spare[0]

    for i in range(count):
        copies[i].wait()
        for p in range(pulse_dev):
            first, last, b = scalars[i, 0, p], scalars[i, 1, p], scalars[i, 2, p]
            x0 = echoes[i][pl.ds(first, tall), :]
            x1 = echoes[i][pl.ds(first + 2, tall), :]
            x2 = echoes[i][pl.ds(last, 8), :]
            keep = lane >= b
            turn = LANES - b
            wide[p * tall : (p + 1) * tall, :] = pltpu.roll(jnp.where(keep, x0, x1), turn, 1)
            end = jnp.where(keep[tall - 8 :], x1[tall - 8 :], x2)
            tail[p * 8 : (p + 1) * 8, :] = pltpu.roll(end, turn, 1)
        for r in range(rows // LANES):
            both = [wide[pl.ds(2 * r + q, pulse_dev, stride=tall), :] for q in range(2)]
            turned[r * LANES : (r + 1) * LANES, :] = jnp.concatenate(both, axis=0).T
        both = [tail[pl.ds(6 + q, pulse_dev, stride=8), :] for q in range(2)]
        turned[rows : rows + 8, :] = jnp.concatenate(both, axis=0).T[:8]

        kern = [jnp.broadcast_to(kerns[i][j : j + 1], (16, 2 * pulse_dev)) for j in range(taps)]
        for f in range(groups):
            base = lax.rem(group + f, groups) * ROW_DEV
            out = outs[f if joined else i * groups + f]
            lanes = slice(i * LANES, (i + 1) * LANES) if joined else slice(0, LANES)

            def fir(m, carry, out=out, lanes=lanes, base=base):
                at = pl.multiple_of(m * 16, 16)
                summed = kern[0] * turned[pl.ds(base + at, 16), :]
                for j in range(1, taps):
                    summed = summed + kern[j] * turned[pl.ds(base + at + j, 16), :]
                out[pl.ds(at, 16), lanes] = summed.astype(jnp.bfloat16)
                return carry

            lax.fori_loop(0, ROW_DEV // 16, fir, 0, unroll=4)


def project_kernel(count, first, *refs):
    pieces, table_ref, out_ref = refs[:count], refs[count], refs[-1]
    left = jnp.concatenate([r[...] for r in pieces], axis=1)
    out_ref[...] = jnp.dot(left, table_ref[first : first + left.shape[1], :], preferred_element_type=jnp.float32)


def finish_kernel(count, first, normaliser, *refs):
    pieces, (table_ref, total_ref, out_hbm, made, sems) = refs[:count], refs[count:]
    left = jnp.concatenate([r[...] for r in pieces], axis=1)
    rows = pl.ds(first, left.shape[1])
    copies = []
    for q in range(2):
        part = slice(q * COL_DEV, (q + 1) * COL_DEV)
        image = jnp.dot(left, table_ref[rows, part], preferred_element_type=jnp.float32)
        made[q] = (image + total_ref[:, part]) * normaliser
        copies.append(pltpu.make_async_copy(made.at[q], out_hbm.at[q], sems.at[q]))
        copies[q].start()
    for copy in copies:
        copy.wait()


def per_device(tiles, groups, echoes, offsets, phase_index, steering, kernels):
    pulse_dev, _, length = echoes.shape
    phases, taps = kernels.shape
    rows = ROW_DEV * groups
    range_rows = length // LANES
    tall = 2 * rows // LANES
    normaliser = (STEPS * pulse_dev * groups) ** (-0.5)
    params = pltpu.CompilerParams(vmem_limit_bytes=24 * 1024 * 1024)

    tile = lax.axis_index("tile")
    odd = tile % 2

    def sent(x, even_by, odd_by, flip):
        pairs = []
        for t in range(tiles):
            for g in range(groups):
                to = ((t + (odd_by if t % 2 else even_by)) % tiles) * groups + (g + flip) % groups
                pairs.append((t * groups + g, to))
        return lax.ppermute(x, ("tile", "pgroup"), pairs)

    def in_pairs(x):
        x = x.reshape(pulse_dev, 2, range_rows, LANES).transpose(0, 2, 1, 3)
        return x.reshape(pulse_dev * range_rows * 2, LANES)

    def spread(x):
        return pl.pallas_call(
            spread_kernel,
            out_shape=jax.ShapeDtypeStruct((pulse_dev * range_rows * 2, LANES), jnp.float32),
            in_specs=[whole()],
            out_specs=whole(),
            compiler_params=params,
            cost_estimate=NOTHING,
            name="spread",
        )(in_pairs(x))

    partner = sent(echoes, 1, -1, 0)
    mine = spread(echoes)
    theirs = in_pairs(partner)
    kern = jnp.broadcast_to(kernels[:, :, None], (phases, taps, 2 * pulse_dev))

    both = jnp.concatenate([offsets, phase_index], axis=0)

    def block_of(block):
        return lax.dynamic_slice_in_dim(both, block % tiles * pulse_dev, pulse_dev, 1)

    ahead = tile + tiles
    blocks = [ahead - 3 + 2 * odd, ahead - 1 - 2 * odd, ahead - 2, tile]
    told = jnp.stack([block_of(block) for block in blocks])
    row = 2 * (told[:, :1] // LANES)
    base = 2 * range_rows * jnp.arange(pulse_dev, dtype=jnp.int32)
    last = jnp.minimum(row + (tall - 4), 2 * range_rows - 8)
    told = jnp.concatenate([base + row, base + last, told[:, :1] % LANES, told[:, 1:]], axis=1)
    told = jnp.concatenate([told, told], axis=2)
    far_ask = sent(told[0], -3, -1, 0)
    ask = sent(told[1:3], -1, -3, 0)

    def profiles(asks, sources, raw, joined):
        count = len(sources)
        shape = jax.ShapeDtypeStruct((ROW_DEV, (count if joined else 1) * 2 * pulse_dev), jnp.bfloat16)
        outs = groups * (1 if joined else count)
        return pl.pallas_call(
            functools.partial(profile_kernel, pulse_dev, rows, taps, phases, groups, raw, joined),
            out_shape=[shape] * outs,
            in_specs=[whole()] * (2 * count + 1),
            out_specs=[whole()] * outs,
            scratch_shapes=[
                pltpu.VMEM((pulse_dev * tall, LANES), jnp.float32),
                pltpu.VMEM((pulse_dev * 8, LANES), jnp.float32),
                pltpu.VMEM((rows + 8, 2 * pulse_dev), jnp.float32),
                pltpu.SMEM((count, 4, 2 * pulse_dev), jnp.int32),
                pltpu.SemaphoreType.DMA((count,)),
            ]
            + [pltpu.VMEM((pulse_dev * 2 * range_rows, LANES), jnp.float32)] * sum(raw),
            compiler_params=params,
            cost_estimate=NOTHING,
            name="profiles",
        )(*asks, kern, *sources)

    near = profiles([ask[0], ask[1]], [mine, theirs], (False, True), True)
    far_ask, *near = lax.optimization_barrier((far_ask, *near))
    near = [sent(near[f], 3, 1, f) for f in range(groups)]
    rest = profiles([far_ask, told[3]], [mine, mine], (False, False), False)
    far = [sent(rest[f], 1, 3, f) for f in range(groups)]
    own = [rest[groups]] + [sent(rest[groups + f], 0, 0, f) for f in range(1, groups)]

    count = STEPS * groups
    table = pl.pallas_call(
        functools.partial(table_kernel, tiles, groups, pulse_dev),
        out_shape=jax.ShapeDtypeStruct((2 * count * pulse_dev, 2 * COL_DEV), jnp.bfloat16),
        in_specs=[whole()],
        out_specs=whole(),
        scratch_shapes=[pltpu.VMEM((2 * count, LANES), jnp.float32)],
        compiler_params=params,
        cost_estimate=NOTHING,
        name="steering_table",
    )(steering[:, 0])

    def project(pieces, first):
        return pl.pallas_call(
            functools.partial(project_kernel, len(pieces), first),
            out_shape=jax.ShapeDtypeStruct((ROW_DEV, 2 * COL_DEV), jnp.float32),
            in_specs=[whole()] * (len(pieces) + 1),
            out_specs=whole(),
            compiler_params=params,
            cost_estimate=NOTHING,
            name="project",
        )(*pieces, table)

    def finish(pieces, first, total):
        return pl.pallas_call(
            functools.partial(finish_kernel, len(pieces), first, normaliser),
            out_shape=jax.ShapeDtypeStruct((2, ROW_DEV, COL_DEV), jnp.float32),
            in_specs=[whole()] * (len(pieces) + 2),
            out_specs=whole(pltpu.HBM),
            scratch_shapes=[pltpu.VMEM((2, ROW_DEV, COL_DEV), jnp.float32), pltpu.SemaphoreType.DMA((2,))],
            compiler_params=params,
            cost_estimate=NOTHING,
            name="finish",
        )(*pieces, table, total)

    wide = 2 * pulse_dev
    total = project(far + own + near[:-1], 0)
    return finish(near[-1:], (4 * groups - 2) * wide, total)


def solution(mesh):
    placed = (
        P(("pgroup", "tile"), None, None),
        P("tile", "pgroup"),
        P("tile", "pgroup"),
        P(None, "tile", None),
        P(),
    )
    body = functools.partial(per_device, mesh.shape["tile"], mesh.shape["pgroup"])
    return jax.shard_map(body, mesh=mesh, in_specs=placed, out_specs=P(None, "pgroup", "tile"), check_vma=False)
```

```python
import functools
import math

import jax
import jax.numpy as jnp
import numpy as np
from jax import lax
from jax.experimental import pallas as pl
from jax.experimental.pallas import tpu as pltpu
from jax.sharding import PartitionSpec as P

ROW_DEV = 256
COL_DEV = 256
STEPS = 4
LANES = 128


def fitted(function, terms):
    nodes = np.cos(np.pi * (np.arange(64) + 0.5) / 64) * 0.25 + 0.25
    values = function(nodes)
    scale = np.vander(nodes * nodes, terms, increasing=True)
    return [float(c) for c in np.linalg.lstsq(scale, values, rcond=None)[0]]


COSINE = fitted(lambda x: np.cos(2 * np.pi * x), 9)
SINE = fitted(lambda x: np.sin(2 * np.pi * x) / x, 8)


def horner(coefficients, z):
    total = jnp.full_like(z, coefficients[-1])
    for c in coefficients[-2::-1]:
        total = total * z + c
    return total


NOTHING = pl.CostEstimate(flops=1, bytes_accessed=1, transcendentals=0)


def whole(space=pltpu.VMEM):
    return pl.BlockSpec(memory_space=space)


def send_order(groups):
    return list(range(groups))[::-1]


def block_twice(ref, row, block, width):
    per = LANES // width
    at = pl.multiple_of(block // per * LANES, LANES)
    line = ref[pl.ds(row, 1), pl.ds(at, LANES)]
    line = pltpu.roll(line, (LANES - block % per * width) % LANES, 1)
    lane = lax.broadcasted_iota(jnp.int32, line.shape, 1)
    return jnp.where(lane < width, line, pltpu.roll(line, width, 1))


def spread_kernel(pairs_ref, spread_ref):
    spread_rows(pairs_ref, spread_ref)


def table_kernel(tiles, groups, pulse_dev, steer_ref, table_ref, lines):
    columns = COL_DEV
    tile, group = lax.axis_index("tile"), lax.axis_index("pgroup")
    count = STEPS * groups
    odd = lax.rem(tile, 2)
    order = send_order(groups)
    slots = [(3 - 2 * odd, f) for f in order]
    slots += [(back, f) for f in order[:-1] for back in (1 + 2 * odd, 2)]
    slots += [(0, f) for f in range(groups)]
    slots += [(back, order[-1]) for back in (1 + 2 * odd, 2)]
    for s, (back, f) in enumerate(slots):
        block = lax.rem(group + (groups - f), groups) * tiles + lax.rem(tile + (tiles - back), tiles)
        for row in range(2):
            at = 2 * s + row
            lines[at : at + 1, :] = block_twice(steer_ref, row, block, pulse_dev)
    upright = lines[...].T
    u = lax.broadcasted_iota(jnp.int32, (1, columns), 1).astype(jnp.float32)
    centred = u - (columns - 1) / 2.0
    linear = centred * (1.0 / (2 * math.pi))
    square = centred * centred * (1.0 / (2 * math.pi * columns))
    for s in range(count):
        rates = upright[:pulse_dev, 2 * s : 2 * s + 1]
        curves = upright[:pulse_dev, 2 * s + 1 : 2 * s + 2]
        turns = rates * linear + curves * square
        x = turns - jnp.round(turns)
        z = x * x
        cosine = horner(COSINE, z)
        sine = horner(SINE, z) * x
        c16 = cosine.astype(jnp.bfloat16)
        s16 = sine.astype(jnp.bfloat16)
        m16 = (-sine).astype(jnp.bfloat16)
        at = 2 * s * pulse_dev
        table_ref[at : at + pulse_dev, :columns] = c16
        table_ref[at : at + pulse_dev, columns:] = s16
        table_ref[at + pulse_dev : at + 2 * pulse_dev, :columns] = m16
        table_ref[at + pulse_dev : at + 2 * pulse_dev, columns:] = c16


def spread_rows(pairs_ref, spread_ref):
    step = 256

    def one(k, carry):
        at = pl.multiple_of(k * step, step)
        spread_ref[pl.ds(at, step), :] = pairs_ref[pl.ds(at, step), :].astype(jnp.float32)
        return carry

    lax.fori_loop(0, pairs_ref.shape[0] // step, one, 0)


def profile_kernel(pulse_dev, rows, taps, phases, groups, raw, joined, *refs):
    count = len(raw)
    asks, kern_ref, refs = refs[:count], refs[count], refs[count + 1 :]
    echoes, refs = list(refs[:count]), refs[count:]
    outs, (wide, tail, turned, scalars, sems, *spare) = refs[: groups * (1 if joined else count)], refs[-5 - raw.count(True) :]
    copies = [pltpu.make_async_copy(asks[i], scalars.at[i], sems.at[i]) for i in range(count)]
    for copy in copies:
        copy.start()
    tall = 2 * rows // LANES
    lane = lax.broadcasted_iota(jnp.int32, (tall, LANES), 1)
    group = lax.axis_index("pgroup")
    kerns = []
    for i in range(count):
        phase = jnp.broadcast_to(asks[i][3:4, :], (taps, 2 * pulse_dev))
        kern = kern_ref[0]
        for h in range(1, phases):
            kern = jnp.where(phase == h, kern_ref[h], kern)
        kerns.append(kern)
        if raw[i]:
            spread_rows(echoes[i], spare[0])
        if raw[i] is not False:
            echoes[i] = spare[0]

    for i in range(count):
        copies[i].wait()
        for p in range(pulse_dev):
            first, last, b = scalars[i, 0, p], scalars[i, 1, p], scalars[i, 2, p]
            x0 = echoes[i][pl.ds(first, tall), :]
            x1 = echoes[i][pl.ds(first + 2, tall), :]
            x2 = echoes[i][pl.ds(last, 8), :]
            keep = lane >= b
            turn = LANES - b
            wide[p * tall : (p + 1) * tall, :] = pltpu.roll(jnp.where(keep, x0, x1), turn, 1)
            end = jnp.where(keep[tall - 8 :], x1[tall - 8 :], x2)
            tail[p * 8 : (p + 1) * 8, :] = pltpu.roll(end, turn, 1)
        for r in range(rows // LANES):
            both = [wide[pl.ds(2 * r + q, pulse_dev, stride=tall), :] for q in range(2)]
            turned[r * LANES : (r + 1) * LANES, :] = jnp.concatenate(both, axis=0).T
        both = [tail[pl.ds(6 + q, pulse_dev, stride=8), :] for q in range(2)]
        turned[rows : rows + 8, :] = jnp.concatenate(both, axis=0).T[:8]

        kern = [jnp.broadcast_to(kerns[i][j : j + 1], (16, 2 * pulse_dev)) for j in range(taps)]
        for f in range(groups):
            base = lax.rem(group + f, groups) * ROW_DEV
            out = outs[f if joined else i * groups + f]
            lanes = slice(i * LANES, (i + 1) * LANES) if joined else slice(0, LANES)

            def fir(m, carry, out=out, lanes=lanes, base=base):
                at = pl.multiple_of(m * 16, 16)
                summed = kern[0] * turned[pl.ds(base + at, 16), :]
                for j in range(1, taps):
                    summed = summed + kern[j] * turned[pl.ds(base + at + j, 16), :]
                out[pl.ds(at, 16), lanes] = summed.astype(jnp.bfloat16)
                return carry

            lax.fori_loop(0, ROW_DEV // 16, fir, 0, unroll=4)


def project_kernel(count, first, *refs):
    pieces, table_ref, out_ref = refs[:count], refs[count], refs[-1]
    left = jnp.concatenate([r[...] for r in pieces], axis=1)
    out_ref[...] = jnp.dot(left, table_ref[first : first + left.shape[1], :], preferred_element_type=jnp.float32)


def finish_kernel(count, first, normaliser, *refs):
    pieces, (table_ref, total_ref, out_hbm, made, sems) = refs[:count], refs[count:]
    left = jnp.concatenate([r[...] for r in pieces], axis=1)
    rows = pl.ds(first, left.shape[1])
    copies = []
    for q in range(2):
        part = slice(q * COL_DEV, (q + 1) * COL_DEV)
        image = jnp.dot(left, table_ref[rows, part], preferred_element_type=jnp.float32)
        made[q] = (image + total_ref[:, part]) * normaliser
        copies.append(pltpu.make_async_copy(made.at[q], out_hbm.at[q], sems.at[q]))
        copies[q].start()
    for copy in copies:
        copy.wait()


def per_device(tiles, groups, echoes, offsets, phase_index, steering, kernels):
    pulse_dev, _, length = echoes.shape
    phases, taps = kernels.shape
    rows = ROW_DEV * groups
    range_rows = length // LANES
    tall = 2 * rows // LANES
    normaliser = (STEPS * pulse_dev * groups) ** (-0.5)
    params = pltpu.CompilerParams(vmem_limit_bytes=24 * 1024 * 1024)

    tile = lax.axis_index("tile")
    odd = tile % 2

    def sent(x, even_by, odd_by, flip):
        pairs = []
        for t in range(tiles):
            for g in range(groups):
                to = ((t + (odd_by if t % 2 else even_by)) % tiles) * groups + (g + flip) % groups
                pairs.append((t * groups + g, to))
        return lax.ppermute(x, ("tile", "pgroup"), pairs)

    def in_pairs(x):
        x = x.reshape(pulse_dev, 2, range_rows, LANES).transpose(0, 2, 1, 3)
        return x.reshape(pulse_dev * range_rows * 2, LANES)

    def spread(x):
        return pl.pallas_call(
            spread_kernel,
            out_shape=jax.ShapeDtypeStruct((pulse_dev * range_rows * 2, LANES), jnp.float32),
            in_specs=[whole()],
            out_specs=whole(),
            compiler_params=params,
            cost_estimate=NOTHING,
            name="spread",
        )(in_pairs(x))

    partner = sent(echoes, 1, -1, 0)
    theirs = spread(partner)
    held, theirs = lax.optimization_barrier((echoes, theirs))
    kern = jnp.broadcast_to(kernels[:, :, None], (phases, taps, 2 * pulse_dev))

    both = jnp.concatenate([offsets, phase_index], axis=0)

    def block_of(block):
        return lax.dynamic_slice_in_dim(both, block % tiles * pulse_dev, pulse_dev, 1)

    ahead = tile + tiles
    blocks = [ahead - 3 + 2 * odd, ahead - 1 - 2 * odd, ahead - 2, tile]
    told = jnp.stack([block_of(block) for block in blocks])
    row = 2 * (told[:, :1] // LANES)
    base = 2 * range_rows * jnp.arange(pulse_dev, dtype=jnp.int32)
    last = jnp.minimum(row + (tall - 4), 2 * range_rows - 8)
    told = jnp.concatenate([base + row, base + last, told[:, :1] % LANES, told[:, 1:]], axis=1)
    told = jnp.concatenate([told, told], axis=2)
    far_ask = sent(told[0], -3, -1, 0)
    ask = sent(told[1:3], -1, -3, 0)

    def profiles(asks, sources, raw, joined):
        count = len(sources)
        shape = jax.ShapeDtypeStruct((ROW_DEV, (count if joined else 1) * 2 * pulse_dev), jnp.bfloat16)
        outs = groups * (1 if joined else count)
        return pl.pallas_call(
            functools.partial(profile_kernel, pulse_dev, rows, taps, phases, groups, raw, joined),
            out_shape=[shape] * outs,
            in_specs=[whole()] * (2 * count + 1),
            out_specs=[whole()] * outs,
            scratch_shapes=[
                pltpu.VMEM((pulse_dev * tall, LANES), jnp.float32),
                pltpu.VMEM((pulse_dev * 8, LANES), jnp.float32),
                pltpu.VMEM((rows + 8, 2 * pulse_dev), jnp.float32),
                pltpu.SMEM((count, 4, 2 * pulse_dev), jnp.int32),
                pltpu.SemaphoreType.DMA((count,)),
            ]
            + [pltpu.VMEM((pulse_dev * 2 * range_rows, LANES), jnp.float32)] * raw.count(True),
            compiler_params=params,
            cost_estimate=NOTHING,
            name="profiles",
        )(*asks, kern, *sources)

    near = profiles([ask[0], ask[1]], [in_pairs(held), theirs], (True, False), True)
    far_ask, *near = lax.optimization_barrier((far_ask, *near))
    near = [sent(near[f], 3, 1, f) for f in range(groups)]
    rest = profiles([far_ask, told[3]], [in_pairs(held)] * 2, (True, None), False)
    far = [sent(rest[f], 1, 3, f) for f in range(groups)]
    own = [rest[groups]] + [sent(rest[groups + f], 0, 0, f) for f in range(1, groups)]

    count = STEPS * groups
    table = pl.pallas_call(
        functools.partial(table_kernel, tiles, groups, pulse_dev),
        out_shape=jax.ShapeDtypeStruct((2 * count * pulse_dev, 2 * COL_DEV), jnp.bfloat16),
        in_specs=[whole()],
        out_specs=whole(),
        scratch_shapes=[pltpu.VMEM((2 * count, LANES), jnp.float32)],
        compiler_params=params,
        cost_estimate=NOTHING,
        name="steering_table",
    )(steering[:, 0])

    def project(pieces, first):
        return pl.pallas_call(
            functools.partial(project_kernel, len(pieces), first),
            out_shape=jax.ShapeDtypeStruct((ROW_DEV, 2 * COL_DEV), jnp.float32),
            in_specs=[whole()] * (len(pieces) + 1),
            out_specs=whole(),
            compiler_params=params,
            cost_estimate=NOTHING,
            name="project",
        )(*pieces, table)

    def finish(pieces, first, total):
        return pl.pallas_call(
            functools.partial(finish_kernel, len(pieces), first, normaliser),
            out_shape=jax.ShapeDtypeStruct((2, ROW_DEV, COL_DEV), jnp.float32),
            in_specs=[whole()] * (len(pieces) + 2),
            out_specs=whole(pltpu.HBM),
            scratch_shapes=[pltpu.VMEM((2, ROW_DEV, COL_DEV), jnp.float32), pltpu.SemaphoreType.DMA((2,))],
            compiler_params=params,
            cost_estimate=NOTHING,
            name="finish",
        )(*pieces, table, total)

    wide = 2 * pulse_dev
    order = send_order(groups)
    total = project([far[f] for f in order] + [near[f] for f in order[:-1]], 0)
    return finish(own + [near[order[-1]]], (3 * groups - 2) * wide, total)


def solution(mesh):
    placed = (
        P(("pgroup", "tile"), None, None),
        P("tile", "pgroup"),
        P("tile", "pgroup"),
        P(None, "tile", None),
        P(),
    )
    body = functools.partial(per_device, mesh.shape["tile"], mesh.shape["pgroup"])
    return jax.shard_map(body, mesh=mesh, in_specs=placed, out_specs=P(None, "pgroup", "tile"), check_vma=False)
```

```python
import functools
import math

import jax
import jax.numpy as jnp
import numpy as np
from jax import lax
from jax.experimental import pallas as pl
from jax.experimental.pallas import tpu as pltpu
from jax.sharding import PartitionSpec as P

ROW_DEV = 256
COL_DEV = 256
STEPS = 4
LANES = 128


def fitted(function, terms):
    nodes = np.cos(np.pi * (np.arange(64) + 0.5) / 64) * 0.25 + 0.25
    values = function(nodes)
    scale = np.vander(nodes * nodes, terms, increasing=True)
    return [float(c) for c in np.linalg.lstsq(scale, values, rcond=None)[0]]


COSINE = fitted(lambda x: np.cos(2 * np.pi * x), 9)
SINE = fitted(lambda x: np.sin(2 * np.pi * x) / x, 8)


def horner(coefficients, z):
    total = jnp.full_like(z, coefficients[-1])
    for c in coefficients[-2::-1]:
        total = total * z + c
    return total


NOTHING = pl.CostEstimate(flops=1, bytes_accessed=1, transcendentals=0)


def whole(space=pltpu.VMEM):
    return pl.BlockSpec(memory_space=space)


def send_order(groups):
    return list(range(groups))[::-1]


def block_twice(ref, row, block, width):
    per = LANES // width
    at = pl.multiple_of(block // per * LANES, LANES)
    line = ref[pl.ds(row, 1), pl.ds(at, LANES)]
    line = pltpu.roll(line, (LANES - block % per * width) % LANES, 1)
    lane = lax.broadcasted_iota(jnp.int32, line.shape, 1)
    return jnp.where(lane < width, line, pltpu.roll(line, width, 1))


def spread_kernel(pairs_ref, spread_ref):
    spread_rows(pairs_ref, spread_ref)


def table_kernel(tiles, groups, pulse_dev, steer_ref, table_ref, lines):
    columns = COL_DEV
    tile, group = lax.axis_index("tile"), lax.axis_index("pgroup")
    count = STEPS * groups
    odd = lax.rem(tile, 2)
    order = send_order(groups)
    slots = [(3 - 2 * odd, f) for f in order]
    slots += [(back, f) for f in order[:-1] for back in (1 + 2 * odd, 2)]
    slots += [(0, f) for f in range(groups)]
    slots += [(back, order[-1]) for back in (1 + 2 * odd, 2)]
    for s, (back, f) in enumerate(slots):
        block = lax.rem(group + (groups - f), groups) * tiles + lax.rem(tile + (tiles - back), tiles)
        for row in range(2):
            at = 2 * s + row
            lines[at : at + 1, :] = block_twice(steer_ref, row, block, pulse_dev)
    upright = lines[...].T
    u = lax.broadcasted_iota(jnp.int32, (1, columns), 1).astype(jnp.float32)
    centred = u - (columns - 1) / 2.0
    linear = centred * (1.0 / (2 * math.pi))
    square = centred * centred * (1.0 / (2 * math.pi * columns))
    for s in range(count):
        rates = upright[:pulse_dev, 2 * s : 2 * s + 1]
        curves = upright[:pulse_dev, 2 * s + 1 : 2 * s + 2]
        turns = rates * linear + curves * square
        x = turns - jnp.round(turns)
        z = x * x
        cosine = horner(COSINE, z)
        sine = horner(SINE, z) * x
        c16 = cosine.astype(jnp.bfloat16)
        s16 = sine.astype(jnp.bfloat16)
        m16 = (-sine).astype(jnp.bfloat16)
        at = 2 * s * pulse_dev
        table_ref[at : at + pulse_dev, :columns] = c16
        table_ref[at : at + pulse_dev, columns:] = s16
        table_ref[at + pulse_dev : at + 2 * pulse_dev, :columns] = m16
        table_ref[at + pulse_dev : at + 2 * pulse_dev, columns:] = c16


def spread_rows(pairs_ref, spread_ref):
    step = 256

    def one(k, carry):
        at = pl.multiple_of(k * step, step)
        spread_ref[pl.ds(at, step), :] = pairs_ref[pl.ds(at, step), :].astype(jnp.float32)
        return carry

    lax.fori_loop(0, pairs_ref.shape[0] // step, one, 0)


def profile_kernel(pulse_dev, rows, taps, phases, groups, raw, joined, *refs):
    count = len(raw)
    asks, kern_ref, refs = refs[:count], refs[count], refs[count + 1 :]
    echoes, refs = list(refs[:count]), refs[count:]
    outs, (wide, tail, turned, scalars, sems, *spare) = refs[: groups * (1 if joined else count)], refs[-5 - raw.count(True) :]
    copies = [pltpu.make_async_copy(asks[i], scalars.at[i], sems.at[i]) for i in range(count)]
    for copy in copies:
        copy.start()
    tall = 2 * rows // LANES
    lane = lax.broadcasted_iota(jnp.int32, (tall, LANES), 1)
    group = lax.axis_index("pgroup")
    kerns = []
    for i in range(count):
        phase = jnp.broadcast_to(asks[i][3:4, :], (taps, 2 * pulse_dev))
        kern = kern_ref[0]
        for h in range(1, phases):
            kern = jnp.where(phase == h, kern_ref[h], kern)
        kerns.append(kern)
        if raw[i]:
            spread_rows(echoes[i], spare[0])
        if raw[i] is not False:
            echoes[i] = spare[0]

    for i in range(count):
        copies[i].wait()
        for p in range(pulse_dev):
            first, last, b = scalars[i, 0, p], scalars[i, 1, p], scalars[i, 2, p]
            x0 = echoes[i][pl.ds(first, tall), :]
            x1 = echoes[i][pl.ds(first + 2, tall), :]
            x2 = echoes[i][pl.ds(last, 8), :]
            keep = lane >= b
            turn = LANES - b
            wide[p * tall : (p + 1) * tall, :] = pltpu.roll(jnp.where(keep, x0, x1), turn, 1)
            end = jnp.where(keep[tall - 8 :], x1[tall - 8 :], x2)
            tail[p * 8 : (p + 1) * 8, :] = pltpu.roll(end, turn, 1)
        for r in range(rows // LANES):
            both = [wide[pl.ds(2 * r + q, pulse_dev, stride=tall), :] for q in range(2)]
            turned[r * LANES : (r + 1) * LANES, :] = jnp.concatenate(both, axis=0).T
        both = [tail[pl.ds(6 + q, pulse_dev, stride=8), :] for q in range(2)]
        turned[rows : rows + 8, :] = jnp.concatenate(both, axis=0).T[:8]

        kern = [jnp.broadcast_to(kerns[i][j : j + 1], (16, 2 * pulse_dev)) for j in range(taps)]
        for f in range(groups):
            base = lax.rem(group + f, groups) * ROW_DEV
            out = outs[f if joined else i * groups + f]
            lanes = slice(i * LANES, (i + 1) * LANES) if joined else slice(0, LANES)

            def fir(m, carry, out=out, lanes=lanes, base=base):
                at = pl.multiple_of(m * 16, 16)
                summed = kern[0] * turned[pl.ds(base + at, 16), :]
                for j in range(1, taps):
                    summed = summed + kern[j] * turned[pl.ds(base + at + j, 16), :]
                out[pl.ds(at, 16), lanes] = summed.astype(jnp.bfloat16)
                return carry

            lax.fori_loop(0, ROW_DEV // 16, fir, 0, unroll=4)


def project_kernel(count, first, *refs):
    pieces, table_ref, out_ref = refs[:count], refs[count], refs[-1]
    left = jnp.concatenate([r[...] for r in pieces], axis=1)
    out_ref[...] = jnp.dot(left, table_ref[first : first + left.shape[1], :], preferred_element_type=jnp.float32)


def finish_kernel(count, first, normaliser, *refs):
    pieces, (table_ref, total_ref, out_hbm, made, sems) = refs[:count], refs[count:]
    left = jnp.concatenate([r[...] for r in pieces], axis=1)
    rows = pl.ds(first, left.shape[1])
    copies = []
    for q in range(2):
        part = slice(q * COL_DEV, (q + 1) * COL_DEV)
        image = jnp.dot(left, table_ref[rows, part], preferred_element_type=jnp.float32)
        made[q] = (image + total_ref[:, part]) * normaliser
        copies.append(pltpu.make_async_copy(made.at[q], out_hbm.at[q], sems.at[q]))
        copies[q].start()
    for copy in copies:
        copy.wait()


def per_device(tiles, groups, echoes, offsets, phase_index, steering, kernels):
    pulse_dev, _, length = echoes.shape
    phases, taps = kernels.shape
    rows = ROW_DEV * groups
    range_rows = length // LANES
    tall = 2 * rows // LANES
    normaliser = (STEPS * pulse_dev * groups) ** (-0.5)
    params = pltpu.CompilerParams(vmem_limit_bytes=24 * 1024 * 1024)

    tile = lax.axis_index("tile")
    odd = tile % 2

    def sent(x, even_by, odd_by, flip):
        pairs = []
        for t in range(tiles):
            for g in range(groups):
                to = ((t + (odd_by if t % 2 else even_by)) % tiles) * groups + (g + flip) % groups
                pairs.append((t * groups + g, to))
        return lax.ppermute(x, ("tile", "pgroup"), pairs)

    def in_pairs(x):
        x = x.reshape(pulse_dev, 2, range_rows, LANES).transpose(0, 2, 1, 3)
        return x.reshape(pulse_dev * range_rows * 2, LANES)

    def spread(x):
        return pl.pallas_call(
            spread_kernel,
            out_shape=jax.ShapeDtypeStruct((pulse_dev * range_rows * 2, LANES), jnp.float32),
            in_specs=[whole()],
            out_specs=whole(),
            compiler_params=params,
            cost_estimate=NOTHING,
            name="spread",
        )(in_pairs(x))

    partner = sent(echoes, 1, -1, 0)
    theirs = spread(partner)
    held, theirs = lax.optimization_barrier((echoes, theirs))
    kern = jnp.broadcast_to(kernels[:, :, None], (phases, taps, 2 * pulse_dev))

    both = jnp.concatenate([offsets, phase_index], axis=0)

    def block_of(block):
        return lax.dynamic_slice_in_dim(both, block % tiles * pulse_dev, pulse_dev, 1)

    ahead = tile + tiles
    blocks = [ahead - 3 + 2 * odd, ahead - 1 - 2 * odd, ahead - 2, tile]
    told = jnp.stack([block_of(block) for block in blocks])
    row = 2 * (told[:, :1] // LANES)
    base = 2 * range_rows * jnp.arange(pulse_dev, dtype=jnp.int32)
    last = jnp.minimum(row + (tall - 4), 2 * range_rows - 8)
    told = jnp.concatenate([base + row, base + last, told[:, :1] % LANES, told[:, 1:]], axis=1)
    told = jnp.concatenate([told, told], axis=2)
    far_ask = sent(told[0], -3, -1, 0)
    ask = sent(told[1:3], -1, -3, 0)

    def profiles(asks, sources, raw, joined):
        count = len(sources)
        shape = jax.ShapeDtypeStruct((ROW_DEV, (count if joined else 1) * 2 * pulse_dev), jnp.bfloat16)
        outs = groups * (1 if joined else count)
        return pl.pallas_call(
            functools.partial(profile_kernel, pulse_dev, rows, taps, phases, groups, raw, joined),
            out_shape=[shape] * outs,
            in_specs=[whole()] * (2 * count + 1),
            out_specs=[whole()] * outs,
            scratch_shapes=[
                pltpu.VMEM((pulse_dev * tall, LANES), jnp.float32),
                pltpu.VMEM((pulse_dev * 8, LANES), jnp.float32),
                pltpu.VMEM((rows + 8, 2 * pulse_dev), jnp.float32),
                pltpu.SMEM((count, 4, 2 * pulse_dev), jnp.int32),
                pltpu.SemaphoreType.DMA((count,)),
            ]
            + [pltpu.VMEM((pulse_dev * 2 * range_rows, LANES), jnp.float32)] * raw.count(True),
            compiler_params=params,
            cost_estimate=NOTHING,
            name="profiles",
        )(*asks, kern, *sources)

    theirs, ask = lax.optimization_barrier((theirs, ask))
    near = profiles([ask[0], ask[1]], [in_pairs(held), theirs], (True, False), True)
    far_ask, *near = lax.optimization_barrier((far_ask, *near))
    near = [sent(near[f], 3, 1, f) for f in range(groups)]
    rest = profiles([far_ask, told[3]], [in_pairs(held)] * 2, (True, None), False)
    far = [sent(rest[f], 1, 3, f) for f in range(groups)]
    own = [rest[groups]] + [sent(rest[groups + f], 0, 0, f) for f in range(1, groups)]

    count = STEPS * groups
    table = pl.pallas_call(
        functools.partial(table_kernel, tiles, groups, pulse_dev),
        out_shape=jax.ShapeDtypeStruct((2 * count * pulse_dev, 2 * COL_DEV), jnp.bfloat16),
        in_specs=[whole()],
        out_specs=whole(),
        scratch_shapes=[pltpu.VMEM((2 * count, LANES), jnp.float32)],
        compiler_params=params,
        cost_estimate=NOTHING,
        name="steering_table",
    )(steering[:, 0])

    def project(pieces, first):
        return pl.pallas_call(
            functools.partial(project_kernel, len(pieces), first),
            out_shape=jax.ShapeDtypeStruct((ROW_DEV, 2 * COL_DEV), jnp.float32),
            in_specs=[whole()] * (len(pieces) + 1),
            out_specs=whole(),
            compiler_params=params,
            cost_estimate=NOTHING,
            name="project",
        )(*pieces, table)

    def finish(pieces, first, total):
        return pl.pallas_call(
            functools.partial(finish_kernel, len(pieces), first, normaliser),
            out_shape=jax.ShapeDtypeStruct((2, ROW_DEV, COL_DEV), jnp.float32),
            in_specs=[whole()] * (len(pieces) + 2),
            out_specs=whole(pltpu.HBM),
            scratch_shapes=[pltpu.VMEM((2, ROW_DEV, COL_DEV), jnp.float32), pltpu.SemaphoreType.DMA((2,))],
            compiler_params=params,
            cost_estimate=NOTHING,
            name="finish",
        )(*pieces, table, total)

    wide = 2 * pulse_dev
    order = send_order(groups)
    total = project([far[f] for f in order] + [near[f] for f in order[:-1]], 0)
    return finish(own + [near[order[-1]]], (3 * groups - 2) * wide, total)


def solution(mesh):
    placed = (
        P(("pgroup", "tile"), None, None),
        P("tile", "pgroup"),
        P("tile", "pgroup"),
        P(None, "tile", None),
        P(),
    )
    body = functools.partial(per_device, mesh.shape["tile"], mesh.shape["pgroup"])
    return jax.shard_map(body, mesh=mesh, in_specs=placed, out_specs=P(None, "pgroup", "tile"), check_vma=False)
```
